256 devices in a mesh: dp: 16 (over y, x), expert: 16 (over z, core).
Axes of the slice: x: 4, y: 4, z: 8, core: 2. Of those that a mesh axis runs over, the one named last changes fastest.
Arguments:
- tokens: bfloat16 [512, 256, 1280], P(('dp', 'expert')), may hold values from -6 to 6, as said below
- router: float32 [1280, 128], replicated
- w_gate: bfloat16 [128, 2560, 1280], P('expert', 'dp'), may hold values from -0.15625 to 0.15625
- w_up: bfloat16 [128, 2560, 1280], P('expert', 'dp'), may hold values from -0.15625 to 0.15625
- w_down: bfloat16 [128, 2560, 1280], P('expert', 'dp'), may hold values from -0.125 to 0.125
Outputs:
- mixed: bfloat16 [512, 256, 1280], P(('dp', 'expert'))
The draws below stay inside these ranges and needn't reach their ends.
Inputs may be any that keep to these rules, and one draw needn't show every extreme that they name: `tokens`: token activations lie in this range.
All inputs are finite; a program needn't handle non-finite values.
Results may differ from the reference program's by a relative error of at most 0.03.
Values may be sent and summed in bfloat16 or wider, within the bound.
No kernel may reach another device: no remote copies, remote signals or barrier semaphores. Data moves between devices by JAX's collectives and lax.ppermute only.
A program may use at most 128 MiB of HBM per device.

```python
import math
import jax
import jax.numpy as jnp
from jax import lax

D = 1280
EXPERTS = 128
FFN_WIDTH = 2560
TOKENS_IMG = 256
IMAGES = 512
HSHARD = 160
N_DP = 16


def shared_parts(key):
    keys = jax.random.split(key, 1)
    normal_base = jax.random.normal(keys[0], (D, EXPERTS), jnp.float32)
    return normal_base


def draw_router(key, part):
    normal_base = shared_parts(key)
    result = jnp.clip(normal_base, -6.0, 6.0) * (3.0 / math.sqrt(D))
    return result.astype(jnp.float32)


def draw_tokens(key, part):
    key = jax.random.fold_in(key, 5)
    first = jax.random.fold_in(key, 0)
    result = jnp.clip(jax.random.normal(first, (IMAGES, TOKENS_IMG, D), jnp.float32), -6.0, 6.0)
    return result.astype(jnp.bfloat16)


def shard_levels(key, dims, shards, smallest, largest):
    def one(axis_at, parts):
        heights = jax.random.uniform(jax.random.fold_in(jax.random.fold_in(key, 6), axis_at), (parts,), jnp.float32, smallest / len(shards), largest / len(shards))
        return jnp.repeat(jnp.exp(heights), dims[axis_at] // parts).reshape((-1,) + (1,) * (len(dims) - axis_at - 1))

    level = one(*shards[0])
    for cut in shards[1:]:
        level = level * one(*cut)
    return level


def gaussian(own_key, dims, scale, most, shards=(), dtype=jnp.bfloat16):
    drawn = scale * jax.random.normal(own_key, dims, jnp.float32)
    if shards:
        drawn = drawn * shard_levels(own_key, dims, shards, -0.22, 0.18)
    return jnp.clip(drawn, -most, most).astype(dtype)


def setup_inputs(seed: int = 0) -> dict:
    key_list = jax.random.split(jax.random.key(seed), 6)
    tokens = draw_tokens(jax.random.fold_in(key_list[5], 71), 0)
    router = draw_router(jax.random.fold_in(key_list[5], 71), 0)
    w_gate = gaussian(key_list[2], (EXPERTS, FFN_WIDTH, D), D ** -0.5, 0.15625, ((0, 16), (1, 16)))
    w_up = gaussian(key_list[3], (EXPERTS, FFN_WIDTH, D), D ** -0.5, 0.15625, ((0, 16), (1, 16)))
    w_down = gaussian(key_list[4], (EXPERTS, FFN_WIDTH, D), FFN_WIDTH ** -0.5, 0.125, ((0, 16), (1, 16)))
    return {"tokens": tokens, "router": router, "w_gate": w_gate, "w_up": w_up, "w_down": w_down}


def one_expert(operands):
    rows, gate_w, up_w, down_w = operands
    gate = jnp.dot(rows, jnp.transpose(gate_w), preferred_element_type=jnp.float32)
    up = jnp.dot(rows, jnp.transpose(up_w), preferred_element_type=jnp.float32)
    act = (jax.nn.silu(gate) * up).astype(jnp.bfloat16)
    blocks = act.reshape(rows.shape[0], N_DP, HSHARD).astype(jnp.float32)
    down_blocks = down_w.reshape(N_DP, HSHARD, D).astype(jnp.float32)
    partial_value = jnp.einsum("bkh,khd->kbd", blocks, down_blocks).astype(jnp.bfloat16)
    partial_value = lax.optimization_barrier(partial_value)
    return jnp.sum(partial_value.astype(jnp.float32), axis=0).astype(jnp.bfloat16)


def reference(tokens, router, w_gate, w_up, w_down):
    tok_f = tokens.astype(jnp.float32)
    logits = jnp.einsum("bmd,de->bme", tok_f, router.astype(jnp.float32))
    dispatch = jax.nn.softmax(logits, axis=1).astype(jnp.bfloat16)
    combine = jax.nn.softmax(logits, axis=2).astype(jnp.bfloat16)
    slots = jnp.einsum("bme,bmd->bed", dispatch.astype(jnp.float32), tok_f).astype(jnp.bfloat16)
    outputs = lax.map(one_expert, (jnp.transpose(slots, (1, 0, 2)), w_gate, w_up, w_down))
    expert_out = jnp.transpose(outputs, (1, 0, 2))
    mixed = jnp.einsum("bme,bed->bmd", combine.astype(jnp.float32), expert_out.astype(jnp.float32))
    return mixed.astype(jnp.bfloat16)
```

```python
import functools

import jax
import jax.numpy as jnp
from jax import lax
from jax.experimental import pallas as pl
from jax.experimental.pallas import tpu as pltpu
from jax.sharding import PartitionSpec as P

D = 1280
EXPERTS = 128
TOK = 256
HS = 160
NDEV = 256
AXES = ("dp", "expert")
F32 = jnp.float32
BF16 = jnp.bfloat16


def place():
    dp = lax.axis_index("dp")
    core = lax.axis_index("expert") & 1
    y, x = dp >> 2, dp & 3
    p = jnp.where(core == 0, x, y)
    q = jnp.where(core == 0, y, x)
    return p, q


def shift_pairs(along_p, by):
    pairs = []
    for y in range(4):
        for x in range(4):
            for e in range(16):
                move_x = (e % 2 == 0) == along_p
                ny, nx = (y, (x + by) % 4) if move_x else ((y + by) % 4, x)
                pairs.append(((y * 4 + x) * 16 + e, (ny * 4 + nx) * 16 + e))
    return pairs


def shift(value, along_p, by):
    return lax.ppermute(value, AXES, shift_pairs(along_p, by))


def row_select(image):
    shape = (EXPERTS, NDEV)
    row = lax.broadcasted_iota(jnp.int32, shape, 1)
    e = lax.broadcasted_iota(jnp.int32, shape, 0)
    y, x, z, core = row >> 6, (row >> 4) & 3, (row >> 1) & 7, row & 1
    p = jnp.where(core == 0, x, y)
    q = jnp.where(core == 0, y, x)
    chosen = z * 16 + core * 8 + p * 2 + (q & 1)
    return jnp.where((chosen == e) & ((q >> 1) == image), 1.0, 0.0).astype(BF16)


def front_kernel(tok_ref, router_ref, rows_ref, comb_ref):
    r = router_ref[...]
    r0 = r.astype(BF16)
    rest = r - r0.astype(F32)
    r1 = rest.astype(BF16)
    r2 = (rest - r1.astype(F32)).astype(BF16)
    rows = jnp.zeros((NDEV, D), F32)
    for i in range(2):
        tok = tok_ref[i]
        logits = (
            jnp.dot(tok, r2, preferred_element_type=F32)
            + jnp.dot(tok, r1, preferred_element_type=F32)
            + jnp.dot(tok, r0, preferred_element_type=F32)
        )
        select = row_select(i)
        ex = jnp.exp(logits - jnp.max(logits, axis=0, keepdims=True))
        disp = (ex / jnp.sum(ex, axis=0, keepdims=True)).astype(BF16)
        ec = jnp.exp(logits - jnp.max(logits, axis=1, keepdims=True))
        comb = (ec / jnp.sum(ec, axis=1, keepdims=True)).astype(BF16)
        disp_rows = jnp.dot(disp, select, preferred_element_type=F32)
        comb_ref[i] = jnp.dot(comb, select, preferred_element_type=F32).astype(BF16)
        rows = rows + jnp.dot(
            jnp.transpose(disp_rows).astype(BF16), tok, preferred_element_type=F32
        )
    rows_ref[...] = rows.astype(BF16)


def front(tokens, router):
    return pl.pallas_call(
        front_kernel,
        out_shape=(
            jax.ShapeDtypeStruct((NDEV, D), BF16),
            jax.ShapeDtypeStruct((2, TOK, NDEV), BF16),
        ),
        in_specs=[pl.BlockSpec(memory_space=pltpu.VMEM)] * 2,
        out_specs=(pl.BlockSpec(memory_space=pltpu.VMEM),) * 2,
        compiler_params=pltpu.CompilerParams(vmem_limit_bytes=40 * 2**20),
        cost_estimate=pl.CostEstimate(flops=900_000_000, bytes_accessed=3_000_000, transcendentals=131072),
    )(tokens, router)


def experts_kernel(
    s0, s2, s1, s3, wg, wu, wd, w1, w2, w3, o0, o2, o1, o3,
    s_buf, gu_buf, wd_buf, o_buf, s_sem, g_sem, u_sem, d_sem, o_sem,
):
    p, q = place()
    odd = q & 1
    slots = (s0, s2, s1, s3)
    outs = (o0, o2, o1, o3)
    moved = (w1, w2, w3)
    copies = []
    for j in range(2):
        pick = odd if j == 0 else 1 - odd
        own = 2 * p + pick
        group = []
        for b in (2 * j, 2 * j + 1):
            group.append(pltpu.make_async_copy(slots[b], s_buf.at[b], s_sem.at[b]))
        for k in range(4):
            if k == 0:
                g, u, d = wg.at[own], wu.at[own], wd.at[own]
            else:
                g, u, d = (moved[k - 1].at[t, pick] for t in range(3))
            lo = pl.ds(k * HS, HS)
            hi = pl.ds(4 * HS + k * HS, HS)
            group.append(pltpu.make_async_copy(g, gu_buf.at[j, lo], g_sem.at[j, k]))
            group.append(pltpu.make_async_copy(u, gu_buf.at[j, hi], u_sem.at[j, k]))
            group.append(pltpu.make_async_copy(d, wd_buf.at[j, lo], d_sem.at[j, k]))
        for c in group:
            c.start()
        copies.append(group)
    out_copies = []
    for j in range(2):
        for c in copies[j]:
            c.wait()

        def block(b, carry, j=j):
            gu = lax.dot_general(
                s_buf[b], gu_buf[j], (((1,), (1,)), ((), ())), preferred_element_type=F32
            )
            gate, up = gu[:, : 4 * HS], gu[:, 4 * HS :]
            act = (gate / (1.0 + jnp.exp(-gate)) * up).astype(BF16)
            o_buf[b] = jnp.dot(act, wd_buf[j], preferred_element_type=F32).astype(BF16)
            return carry

        lax.fori_loop(2 * j, 2 * j + 2, block, 0)
        for b in (2 * j, 2 * j + 1):
            c = pltpu.make_async_copy(o_buf.at[b], outs[b], o_sem.at[b])
            c.start()
            out_copies.append(c)
    for c in out_copies:
        c.wait()


def experts(s0, s2, s1, s3, wg, wu, wd, w1, w2, w3):
    block = jax.ShapeDtypeStruct((NDEV, D), BF16)
    return pl.pallas_call(
        experts_kernel,
        out_shape=(block,) * 4,
        in_specs=[pl.BlockSpec(memory_space=pl.ANY)] * 10,
        out_specs=(pl.BlockSpec(memory_space=pl.ANY),) * 4,
        scratch_shapes=[
            pltpu.VMEM((4, NDEV, D), BF16),
            pltpu.VMEM((2, 8 * HS, D), BF16),
            pltpu.VMEM((2, 4 * HS, D), BF16),
            pltpu.VMEM((4, NDEV, D), BF16),
            pltpu.SemaphoreType.DMA((4,)),
            pltpu.SemaphoreType.DMA((2, 4)),
            pltpu.SemaphoreType.DMA((2, 4)),
            pltpu.SemaphoreType.DMA((2, 4)),
            pltpu.SemaphoreType.DMA((4,)),
        ],
        compiler_params=pltpu.CompilerParams(vmem_limit_bytes=44 * 2**20),
        cost_estimate=pl.CostEstimate(flops=5_100_000_000, bytes_accessed=15_000_000, transcendentals=1310720),
    )(s0, s2, s1, s3, wg, wu, wd, w1, w2, w3)


def body(tokens, router, w_gate, w_up, w_down):
    p, _ = place()

    def moved(by):
        first = 2 * ((p + by) & 3)
        parts = [lax.dynamic_slice_in_dim(w, first, 2, 0) for w in (w_gate, w_up, w_down)]
        return shift(jnp.stack(parts), True, by)

    w1, w3, w2 = moved(1), moved(3), moved(2)
    rows, comb = front(tokens, router)
    s0 = lax.all_to_all(rows, AXES, split_axis=0, concat_axis=0, tiled=True)
    s1, s3, s2 = (shift(s0, False, by) for by in (1, 3, 2))
    o0, o2, o1, o3 = experts(s0, s2, s1, s3, w_gate, w_up, w_down, w1, w2, w3)
    t1, t3, t2 = shift(o1, False, 3), shift(o3, False, 1), shift(o2, False, 2)
    total = o0.astype(F32) + t1.astype(F32) + t2.astype(F32) + t3.astype(F32)
    out_rows = lax.all_to_all(
        total.astype(BF16), AXES, split_axis=0, concat_axis=0, tiled=True
    )
    mixed = jnp.dot(comb.reshape(2 * TOK, NDEV), out_rows, preferred_element_type=F32)
    return mixed.astype(BF16).reshape(2, TOK, D)


def solution(mesh):
    return jax.shard_map(
        body,
        mesh=mesh,
        in_specs=(
            P(("dp", "expert"), None, None),
            P(),
            P("expert", "dp", None),
            P("expert", "dp", None),
            P("expert", "dp", None),
        ),
        out_specs=P(("dp", "expert"), None, None),
        check_vma=False,
    )
```

```python
import functools

import jax
import jax.numpy as jnp
from jax import lax
from jax.experimental import pallas as pl
from jax.experimental.pallas import tpu as pltpu
from jax.sharding import PartitionSpec as P

D = 1280
EXPERTS = 128
TOK = 256
HS = 160
ROWS = 256
AXES = ("dp", "expert")
F32 = jnp.float32
BF16 = jnp.bfloat16


def place():
    dp = lax.axis_index("dp")
    core = lax.axis_index("expert") & 1
    y, x = dp >> 2, dp & 3
    p = jnp.where(core == 0, x, y)
    q = jnp.where(core == 0, y, x)
    return p, q


def shift_pairs(along_p, by):
    pairs = []
    for y in range(4):
        for x in range(4):
            for e in range(16):
                move_x = (e % 2 == 0) == along_p
                ny, nx = (y, (x + by) % 4) if move_x else ((y + by) % 4, x)
                pairs.append(((y * 4 + x) * 16 + e, (ny * 4 + nx) * 16 + e))
    return pairs


def shift(value, along_p, by):
    return lax.ppermute(value, AXES, shift_pairs(along_p, by))


def row_select(image):
    shape = (EXPERTS, ROWS)
    row = lax.broadcasted_iota(jnp.int32, shape, 1)
    e = lax.broadcasted_iota(jnp.int32, shape, 0)
    y, x, z, core = row >> 6, (row >> 4) & 3, (row >> 1) & 7, row & 1
    p = jnp.where(core == 0, x, y)
    q = jnp.where(core == 0, y, x)
    chosen = z * 16 + core * 8 + p * 2 + (q & 1)
    return jnp.where((chosen == e) & ((q >> 1) == image), 1.0, 0.0).astype(BF16)


def front_kernel(tok_ref, router_ref, rows_ref, comb_ref):
    r = router_ref[...]
    r0 = r.astype(BF16)
    rest = r - r0.astype(F32)
    r1 = rest.astype(BF16)
    r2 = (rest - r1.astype(F32)).astype(BF16)
    rows = jnp.zeros((ROWS, D), F32)
    for i in range(2):
        tok = tok_ref[i]
        logits = (
            jnp.dot(tok, r2, preferred_element_type=F32)
            + jnp.dot(tok, r1, preferred_element_type=F32)
            + jnp.dot(tok, r0, preferred_element_type=F32)
        )
        select = row_select(i)
        ex = jnp.exp(logits - jnp.max(logits, axis=0, keepdims=True))
        disp = (ex / jnp.sum(ex, axis=0, keepdims=True)).astype(BF16)
        ec = jnp.exp(logits - jnp.max(logits, axis=1, keepdims=True))
        comb = (ec / jnp.sum(ec, axis=1, keepdims=True)).astype(BF16)
        disp_rows = jnp.dot(disp, select, preferred_element_type=F32)
        comb_ref[i] = jnp.dot(comb, select, preferred_element_type=F32).astype(BF16)
        rows = rows + jnp.dot(
            jnp.transpose(disp_rows).astype(BF16), tok, preferred_element_type=F32
        )
    rows_ref[...] = rows.astype(BF16)


def front(tokens, router):
    return pl.pallas_call(
        front_kernel,
        out_shape=(
            jax.ShapeDtypeStruct((ROWS, D), BF16),
            jax.ShapeDtypeStruct((2, TOK, ROWS), BF16),
        ),
        in_specs=[pl.BlockSpec(memory_space=pltpu.VMEM)] * 2,
        out_specs=(pl.BlockSpec(memory_space=pltpu.VMEM),) * 2,
        compiler_params=pltpu.CompilerParams(vmem_limit_bytes=20 * 2**20),
        cost_estimate=pl.CostEstimate(flops=900_000_000, bytes_accessed=3_000_000, transcendentals=131072),
    )(tokens, router)


def pack_kernel(plans, *refs):
    weights, outs, (buf, in_sem, out_sem) = refs[:3], refs[3 : 3 + len(plans)], refs[3 + len(plans) :]
    p, _ = place()
    loads, stores = [], []
    slot = 0
    for (by, which), out in zip(plans, outs):
        there = pl.ds(2 * ((p + by) & 3), 2)
        for n, t in enumerate(which):
            loads.append(pltpu.make_async_copy(weights[t].at[there], buf.at[slot], in_sem.at[slot]))
            stores.append(pltpu.make_async_copy(buf.at[slot], out.at[n], out_sem.at[slot]))
            slot += 1
    for c in loads:
        c.start()
    for load, store in zip(loads, stores):
        load.wait()
        store.start()
    for c in stores:
        c.wait()


def pack(weights, plans):
    slots = sum(len(which) for _, which in plans)
    return pl.pallas_call(
        functools.partial(pack_kernel, plans),
        out_shape=tuple(jax.ShapeDtypeStruct((len(which), 2, HS, D), BF16) for _, which in plans),
        in_specs=[pl.BlockSpec(memory_space=pl.ANY)] * 3,
        out_specs=(pl.BlockSpec(memory_space=pl.ANY),) * len(plans),
        scratch_shapes=[
            pltpu.VMEM((slots, 2, HS, D), BF16),
            pltpu.SemaphoreType.DMA((slots,)),
            pltpu.SemaphoreType.DMA((slots,)),
        ],
        compiler_params=pltpu.CompilerParams(vmem_limit_bytes=16 * 2**20),
        cost_estimate=pl.CostEstimate(flops=0, bytes_accessed=slots * 1_640_000, transcendentals=0),
    )(*in_hbm(weights))


def in_hbm(arrays):
    return [pltpu.with_memory_space_constraint(a, pltpu.HBM) for a in arrays]


def collect_kernel(wg, wu, wd, a1, a2, a3, b1, b2, b3, gu1, wd1, gu2, wd2, sems):
    p, q = place()
    copies = []
    for j, (gu_ref, wd_ref) in enumerate(((gu1, wd1), (gu2, wd2))):
        pick = (q & 1) ^ j
        own = 2 * p + pick
        sources = (
            (wg.at[own], wu.at[own], wd.at[own]),
        ) + tuple(
            (a.at[0, pick], a.at[1, pick], b.at[0, pick])
            for a, b in ((a1, b1), (a2, b2), (a3, b3))
        )
        for k, (g, u, d) in enumerate(sources):
            lo = pl.ds(k * HS, HS)
            hi = pl.ds(4 * HS + k * HS, HS)
            copies.append(pltpu.make_async_copy(g, gu_ref.at[lo], sems.at[j, 0, k]))
            copies.append(pltpu.make_async_copy(u, gu_ref.at[hi], sems.at[j, 1, k]))
            copies.append(pltpu.make_async_copy(d, wd_ref.at[lo], sems.at[j, 2, k]))
    for c in copies:
        c.start()
    for c in copies:
        c.wait()


def collect(weights, moved):
    gu = jax.ShapeDtypeStruct((8 * HS, D), BF16)
    down = jax.ShapeDtypeStruct((4 * HS, D), BF16)
    return pl.pallas_call(
        collect_kernel,
        out_shape=(gu, down, gu, down),
        in_specs=[pl.BlockSpec(memory_space=pl.ANY)] * 9,
        out_specs=(pl.BlockSpec(memory_space=pltpu.VMEM),) * 4,
        scratch_shapes=[pltpu.SemaphoreType.DMA((2, 3, 4))],
        compiler_params=pltpu.CompilerParams(vmem_limit_bytes=16 * 2**20),
        cost_estimate=pl.CostEstimate(flops=0, bytes_accessed=10_000_000, transcendentals=0),
    )(*in_hbm(weights), *moved)


def expert_kernel(sa, sb, gu_ref, wd_ref, oa, ob):
    rows = jnp.concatenate([sa[...], sb[...]], axis=0)
    gu = lax.dot_general(rows, gu_ref[...], (((1,), (1,)), ((), ())), preferred_element_type=F32)
    gate, up = gu[:, : 4 * HS], gu[:, 4 * HS :]
    act = (gate / (1.0 + jnp.exp(-gate)) * up).astype(BF16)
    out = jnp.dot(act, wd_ref[...], preferred_element_type=F32).astype(BF16)
    oa[...] = out[:ROWS]
    ob[...] = out[ROWS:]


def expert(sa, sb, gu, down):
    block = jax.ShapeDtypeStruct((ROWS, D), BF16)
    return pl.pallas_call(
        expert_kernel,
        out_shape=(block,) * 2,
        in_specs=[pl.BlockSpec(memory_space=pltpu.VMEM)] * 4,
        out_specs=(pl.BlockSpec(memory_space=pltpu.VMEM),) * 2,
        compiler_params=pltpu.CompilerParams(vmem_limit_bytes=24 * 2**20),
        cost_estimate=pl.CostEstimate(
            flops=2_500_000_000, bytes_accessed=2_000_000, transcendentals=655360
        ),
    )(sa, sb, gu, down)


def body(tokens, router, w_gate, w_up, w_down):
    weights = (w_gate, w_up, w_down)
    ups = pack(weights, tuple((by, (0, 1)) for by in (1, 2, 3)))
    tokens, router, *ups = lax.optimization_barrier((tokens, router, *ups))
    rows, comb = front(tokens, router)
    ups = [shift(w, True, by) for w, by in zip(ups, (1, 2, 3))]
    downs = pack(weights, tuple((by, (2,)) for by in (1, 2, 3)))
    downs = [shift(w, True, by) for w, by in zip(downs, (1, 2, 3))]
    s0 = lax.all_to_all(rows, AXES, split_axis=0, concat_axis=0, tiled=True)
    s0, *ups = lax.optimization_barrier((s0, *ups))
    s2, s1, s3 = (shift(s0, False, by) for by in (2, 1, 3))
    gu1, down1, gu2, down2 = collect(weights, ups + downs)
    o2, o0 = expert(s2, s0, gu1, down1)
    s1, s3, o2 = lax.optimization_barrier((s1, s3, o2))
    o1, o3 = expert(s1, s3, gu2, down2)
    t2, t1, t3 = shift(o2, False, 2), shift(o1, False, 3), shift(o3, False, 1)
    total = o0.astype(F32) + t1.astype(F32) + t2.astype(F32) + t3.astype(F32)
    out_rows = lax.all_to_all(
        total.astype(BF16), AXES, split_axis=0, concat_axis=0, tiled=True
    )
    mixed = jnp.dot(comb.reshape(2 * TOK, ROWS), out_rows, preferred_element_type=F32)
    return mixed.astype(BF16).reshape(2, TOK, D)


def solution(mesh):
    return jax.shard_map(
        body,
        mesh=mesh,
        in_specs=(
            P(("dp", "expert"), None, None),
            P(),
            P("expert", "dp", None),
            P("expert", "dp", None),
            P("expert", "dp", None),
        ),
        out_specs=P(("dp", "expert"), None, None),
        check_vma=False,
    )
```

```python
import functools
import math

import jax
import jax.numpy as jnp
from jax import lax
from jax.experimental import pallas as pl
from jax.experimental.pallas import tpu as pltpu
from jax.sharding import PartitionSpec as P

D = 1280
EXPERTS = 128
TOK = 256
HS = 160
ROWS = 256
AXES = ("dp", "expert")
F32 = jnp.float32
BF16 = jnp.bfloat16


def place():
    dp = lax.axis_index("dp")
    core = lax.axis_index("expert") & 1
    y, x = dp >> 2, dp & 3
    p = jnp.where(core == 0, x, y)
    q = jnp.where(core == 0, y, x)
    return p, q


def shift_pairs(along_p, by):
    pairs = []
    for y in range(4):
        for x in range(4):
            for e in range(16):
                move_x = (e % 2 == 0) == along_p
                ny, nx = (y, (x + by) % 4) if move_x else ((y + by) % 4, x)
                pairs.append(((y * 4 + x) * 16 + e, (ny * 4 + nx) * 16 + e))
    return pairs


GROUPS = [
    [
        ((f * 4 + p) if core == 0 else (p * 4 + f)) * 16 + z * 2 + core
        for p in range(4)
        for z in range(8)
    ]
    for core in range(2)
    for f in range(4)
]


def exchange(rows):
    return lax.all_to_all(
        rows, AXES, split_axis=0, concat_axis=0, tiled=True, axis_index_groups=GROUPS
    )


def swap(value):
    return lax.ppermute(value, "expert", [(e, e ^ 1) for e in range(16)])


def shift(value, along_p, by):
    return lax.ppermute(value, AXES, shift_pairs(along_p, by))


def one_hot(chosen, lines):
    line = lax.broadcasted_iota(jnp.int32, (lines, ROWS), 0)
    return jnp.where(chosen == line, 1.0, 0.0).astype(BF16)


def columns(lines):
    return lax.broadcasted_iota(jnp.int32, (lines, ROWS), 1)


def front_kernel(tok_ref, router_ref, mine_ref, other_ref, comb_ref):
    row = columns(EXPERTS)
    core = (lax.axis_index("expert") & 1) ^ (row >> 7)
    expert = ((row >> 2) & 7) * 16 + core * 8 + ((row >> 5) & 3) * 2 + ((row >> 1) & 1)
    r = router_ref[...]
    r0 = r.astype(BF16)
    rest = r - r0.astype(F32)
    r1 = rest.astype(BF16)
    r2 = (rest - r1.astype(F32)).astype(BF16)
    rows = jnp.zeros((ROWS, D), F32)
    for i in range(2):
        tok = tok_ref[i]
        logits = (
            jnp.dot(tok, r2, preferred_element_type=F32)
            + jnp.dot(tok, r1, preferred_element_type=F32)
            + jnp.dot(tok, r0, preferred_element_type=F32)
        )
        select = one_hot(jnp.where((row & 1) == i, expert, -1), EXPERTS)
        ex = jnp.exp(logits - jnp.max(logits, axis=0, keepdims=True))
        disp = (ex / jnp.sum(ex, axis=0, keepdims=True)).astype(BF16)
        ec = jnp.exp(logits - jnp.max(logits, axis=1, keepdims=True))
        comb = (ec / jnp.sum(ec, axis=1, keepdims=True)).astype(BF16)
        disp_rows = jnp.dot(disp, select, preferred_element_type=F32)
        comb_ref[i] = jnp.dot(comb, select, preferred_element_type=F32).astype(BF16)
        rows = rows + jnp.dot(
            jnp.transpose(disp_rows).astype(BF16), tok, preferred_element_type=F32
        )
    mine_ref[...] = rows[:128].astype(BF16)
    other_ref[...] = rows[128:].astype(BF16)


def front(tokens, router):
    return pl.pallas_call(
        front_kernel,
        out_shape=(
            jax.ShapeDtypeStruct((128, D), BF16),
            jax.ShapeDtypeStruct((128, D), BF16),
            jax.ShapeDtypeStruct((2, TOK, ROWS), BF16),
        ),
        in_specs=[pl.BlockSpec(memory_space=pltpu.VMEM)] * 2,
        out_specs=(pl.BlockSpec(memory_space=pltpu.VMEM),) * 3,
        compiler_params=pltpu.CompilerParams(vmem_limit_bytes=20 * 2**20),
        cost_estimate=pl.CostEstimate(flops=900_000_000, bytes_accessed=3_000_000, transcendentals=131072),
    )(tokens, router)


def pack_kernel(plans, *refs):
    weights, outs, (buf, in_sem, out_sem) = refs[:3], refs[3 : 3 + len(plans)], refs[3 + len(plans) :]
    p, _ = place()
    loads, stores = [], []
    slot = 0
    for (by, which), out in zip(plans, outs):
        there = pl.ds(2 * ((p + by) & 3), 2)
        for n, t in enumerate(which):
            loads.append(pltpu.make_async_copy(weights[t].at[there], buf.at[slot], in_sem.at[slot]))
            stores.append(pltpu.make_async_copy(buf.at[slot], out.at[n], out_sem.at[slot]))
            slot += 1
    for c in loads:
        c.start()
    for load, store in zip(loads, stores):
        load.wait()
        store.start()
    for c in stores:
        c.wait()


def pack(weights, plans):
    slots = sum(len(which) for _, which in plans)
    return pl.pallas_call(
        functools.partial(pack_kernel, plans),
        out_shape=tuple(jax.ShapeDtypeStruct((len(which), 2, HS, D), BF16) for _, which in plans),
        in_specs=[pl.BlockSpec(memory_space=pl.ANY)] * 3,
        out_specs=(pl.BlockSpec(memory_space=pl.ANY),) * len(plans),
        scratch_shapes=[
            pltpu.VMEM((slots, 2, HS, D), BF16),
            pltpu.SemaphoreType.DMA((slots,)),
            pltpu.SemaphoreType.DMA((slots,)),
        ],
        compiler_params=pltpu.CompilerParams(vmem_limit_bytes=16 * 2**20),
        cost_estimate=pl.CostEstimate(flops=0, bytes_accessed=slots * 1_640_000, transcendentals=0),
    )(*in_hbm(weights))


def in_hbm(arrays):
    return [pltpu.with_memory_space_constraint(a, pltpu.HBM) for a in arrays]


def reorder_kernel(source, count, *refs):
    parts, outs = refs[:count], refs[count:]
    rows = jnp.concatenate([r[...].reshape(-1, D) for r in parts], axis=0)
    moved = lax.dot_general(
        one_hot(source(columns(ROWS)), ROWS),
        rows,
        (((0,), (0,)), ((), ())),
        preferred_element_type=F32,
    ).astype(BF16)
    start = 0
    for out in outs:
        size = math.prod(out.shape[:-1])
        out[...] = moved[start : start + size].reshape(out.shape)
        start += size


def reorder(parts, source, shapes):
    return pl.pallas_call(
        functools.partial(reorder_kernel, source, len(parts)),
        out_shape=tuple(jax.ShapeDtypeStruct(shape, BF16) for shape in shapes),
        in_specs=[pl.BlockSpec(memory_space=pltpu.VMEM)] * len(parts),
        out_specs=(pl.BlockSpec(memory_space=pltpu.VMEM),) * len(shapes),
        compiler_params=pltpu.CompilerParams(vmem_limit_bytes=16 * 2**20),
        cost_estimate=pl.CostEstimate(flops=170_000_000, bytes_accessed=1_300_000, transcendentals=0),
    )(*parts)


def weave(n):
    return ((n >> 2) & 1) * 128 + (n >> 3) * 4 + (n & 3)


def unweave(n):
    return ((n >> 2) & 31) * 8 + (n >> 7) * 4 + (n & 3)


def deal(n):
    return ((n >> 2) & 31) * 8 + ((n >> 1) & 1) * 4 + (n >> 7) * 2 + (n & 1)


def undeal(n):
    return ((n >> 1) & 1) * 128 + (n >> 3) * 4 + ((n >> 2) & 1) * 2 + (n & 1)


def collect_kernel(*refs):
    weights, moved, (out, sems) = refs[:-5], refs[-5:-2], refs[-2:]
    p, _ = place()
    copies = []
    for j in range(2):
        for t, w in enumerate(weights):
            sources = [w.at[2 * p + j]] + [m.at[t, j] for m in moved]
            for k, src in enumerate(sources):
                dst = out.at[j, pl.ds((4 * t + k) * HS, HS)]
                copies.append(pltpu.make_async_copy(src, dst, sems.at[j, t, k]))
    for c in copies:
        c.start()
    for c in copies:
        c.wait()


def collect(weights, moved):
    count = len(weights)
    return pl.pallas_call(
        collect_kernel,
        out_shape=jax.ShapeDtypeStruct((2, count * 4 * HS, D), BF16),
        in_specs=[pl.BlockSpec(memory_space=pl.ANY)] * (count + 3),
        out_specs=pl.BlockSpec(memory_space=pltpu.VMEM),
        scratch_shapes=[pltpu.SemaphoreType.DMA((2, count, 4))],
        compiler_params=pltpu.CompilerParams(vmem_limit_bytes=16 * 2**20),
        cost_estimate=pl.CostEstimate(flops=0, bytes_accessed=count * 6_600_000, transcendentals=0),
    )(*in_hbm(weights), *moved)


def experts_kernel(count, *refs):
    slots, (gu_ref, wd_ref), outs = refs[:count], refs[count : count + 2], refs[count + 2 :]
    for j in range(2):
        rows = jnp.concatenate([s[j] for s in slots], axis=0)
        gu = lax.dot_general(
            rows, gu_ref[j], (((1,), (1,)), ((), ())), preferred_element_type=F32
        )
        gate, up = gu[:, : 4 * HS], gu[:, 4 * HS :]
        act = (gate / (1.0 + jnp.exp(-gate)) * up).astype(BF16)
        out = jnp.dot(act, wd_ref[j], preferred_element_type=F32).astype(BF16)
        start = 0
        for o in outs:
            o[j] = out[start : start + o.shape[1]]
            start += o.shape[1]


def experts(slots, gu, down):
    rows = sum(2 * s.shape[1] for s in slots)
    return pl.pallas_call(
        functools.partial(experts_kernel, len(slots)),
        out_shape=tuple(jax.ShapeDtypeStruct(s.shape, BF16) for s in slots),
        in_specs=[pl.BlockSpec(memory_space=pltpu.VMEM)] * (len(slots) + 2),
        out_specs=(pl.BlockSpec(memory_space=pltpu.VMEM),) * len(slots),
        compiler_params=pltpu.CompilerParams(vmem_limit_bytes=24 * 2**20),
        cost_estimate=pl.CostEstimate(
            flops=rows * 4_900_000, bytes_accessed=2_000_000, transcendentals=rows * 1280
        ),
    )(*slots, gu, down)


def merge_kernel(o1, o3, x, y, out1, out3):
    half = x.shape[1]
    out3[:, :half] = (o3[:, :half].astype(F32) + x[...].astype(F32)).astype(BF16)
    out3[:, half:] = o3[:, half:]
    out1[:, :half] = o1[:, :half]
    out1[:, half:] = (o1[:, half:].astype(F32) + y[...].astype(F32)).astype(BF16)


def merge(o1, o3, x, y):
    return pl.pallas_call(
        merge_kernel,
        out_shape=(jax.ShapeDtypeStruct(o1.shape, BF16),) * 2,
        in_specs=[pl.BlockSpec(memory_space=pltpu.VMEM)] * 4,
        out_specs=(pl.BlockSpec(memory_space=pltpu.VMEM),) * 2,
        compiler_params=pltpu.CompilerParams(vmem_limit_bytes=8 * 2**20),
        cost_estimate=pl.CostEstimate(flops=400_000, bytes_accessed=3_000_000, transcendentals=0),
    )(o1, o3, x, y)


def body(tokens, router, w_gate, w_up, w_down):
    ups = pack((w_gate, w_up, w_down), tuple((by, (0, 1)) for by in (1, 2, 3)))
    tokens, router, *ups = lax.optimization_barrier((tokens, router, *ups))
    mine, other, comb = front(tokens, router)
    ups = [shift(w, True, by) for w, by in zip(ups, (1, 2, 3))]
    downs = pack((w_gate, w_up, w_down), tuple((by, (2,)) for by in (1, 2, 3)))
    downs = [shift(w, True, by) for w, by in zip(downs, (1, 2, 3))]
    (rows,) = reorder((mine, swap(other)), weave, ((ROWS, D),))
    rows = exchange(rows)
    rows, *ups = lax.optimization_barrier((rows, *ups))
    (s0,) = reorder((rows,), deal, ((2, 128, D),))
    s1, s3 = shift(s0, False, 1), shift(s0, False, 3)
    gu = collect((w_gate, w_up), ups)
    s1, s3, gu = lax.optimization_barrier((s1, s3, gu))
    far = shift(s1[:, :64], False, 1), shift(s3[:, 64:], False, 3)
    down = collect((w_down,), downs)
    o1, o3 = experts((s1, s3), gu, down)
    far, o1, o3 = lax.optimization_barrier((far, o1, o3))
    low, high = experts(far, gu, down)
    x, y = shift(low, False, 1), shift(high, False, 3)
    (o0,) = experts((s0,), gu, down)
    o1, o3 = merge(o1, o3, x, y)
    t1, t3 = shift(o1, False, 3), shift(o3, False, 1)
    total = o0.astype(F32) + t1.astype(F32) + t3.astype(F32)
    (rows,) = reorder((total.astype(BF16),), undeal, ((ROWS, D),))
    mine, other = reorder((exchange(rows),), unweave, ((128, D),) * 2)
    rows = jnp.concatenate([mine, swap(other)], axis=0)
    mixed = jnp.dot(comb.reshape(2 * TOK, ROWS), rows, preferred_element_type=F32)
    return mixed.astype(BF16).reshape(2, TOK, D)


def solution(mesh):
    return jax.shard_map(
        body,
        mesh=mesh,
        in_specs=(
            P(("dp", "expert"), None, None),
            P(),
            P("expert", "dp", None),
            P("expert", "dp", None),
            P("expert", "dp", None),
        ),
        out_specs=P(("dp", "expert"), None, None),
        check_vma=False,
    )
```

```python
import functools
import math

import jax
import jax.numpy as jnp
from jax import lax
from jax.experimental import pallas as pl
from jax.experimental.pallas import tpu as pltpu
from jax.sharding import PartitionSpec as P

D = 1280
EXPERTS = 128
TOK = 256
HS = 160
ROWS = 256
AXES = ("dp", "expert")
F32 = jnp.float32
BF16 = jnp.bfloat16


def place():
    dp = lax.axis_index("dp")
    core = lax.axis_index("expert") & 1
    y, x = dp >> 2, dp & 3
    p = jnp.where(core == 0, x, y)
    q = jnp.where(core == 0, y, x)
    return p, q


def shift_pairs(along_p, by):
    pairs = []
    for y in range(4):
        for x in range(4):
            for e in range(16):
                move_x = (e % 2 == 0) == along_p
                ny, nx = (y, (x + by) % 4) if move_x else ((y + by) % 4, x)
                pairs.append(((y * 4 + x) * 16 + e, (ny * 4 + nx) * 16 + e))
    return pairs


GROUPS = [
    [
        ((f * 4 + p) if core == 0 else (p * 4 + f)) * 16 + z * 2 + core
        for p in range(4)
        for z in range(8)
    ]
    for core in range(2)
    for f in range(4)
]


def exchange(rows):
    return lax.all_to_all(
        rows, AXES, split_axis=0, concat_axis=0, tiled=True, axis_index_groups=GROUPS
    )


def swap(value):
    return lax.ppermute(value, "expert", [(e, e ^ 1) for e in range(16)])


def shift(value, along_p, by):
    return lax.ppermute(value, AXES, shift_pairs(along_p, by))


def one_hot(chosen, lines):
    line = lax.broadcasted_iota(jnp.int32, (lines, ROWS), 0)
    return jnp.where(chosen == line, 1.0, 0.0).astype(BF16)


def columns(lines):
    return lax.broadcasted_iota(jnp.int32, (lines, ROWS), 1)


def front_kernel(tok_ref, router_ref, mine_ref, other_ref, comb_ref):
    row = columns(EXPERTS)
    core = (lax.axis_index("expert") & 1) ^ (row >> 7)
    expert = ((row >> 2) & 7) * 16 + core * 8 + ((row >> 5) & 3) * 2 + ((row >> 1) & 1)
    r = router_ref[...]
    r0 = r.astype(BF16)
    rest = r - r0.astype(F32)
    r1 = rest.astype(BF16)
    r2 = (rest - r1.astype(F32)).astype(BF16)
    rows = jnp.zeros((ROWS, D), F32)
    for i in range(2):
        tok = tok_ref[i]
        logits = (
            jnp.dot(tok, r2, preferred_element_type=F32)
            + jnp.dot(tok, r1, preferred_element_type=F32)
            + jnp.dot(tok, r0, preferred_element_type=F32)
        )
        select = one_hot(jnp.where((row & 1) == i, expert, -1), EXPERTS)
        ex = jnp.exp(logits - jnp.max(logits, axis=0, keepdims=True))
        disp = (ex / jnp.sum(ex, axis=0, keepdims=True)).astype(BF16)
        ec = jnp.exp(logits - jnp.max(logits, axis=1, keepdims=True))
        comb = (ec / jnp.sum(ec, axis=1, keepdims=True)).astype(BF16)
        disp_rows = jnp.dot(disp, select, preferred_element_type=F32)
        comb_ref[i] = jnp.dot(comb, select, preferred_element_type=F32).astype(BF16)
        rows = rows + jnp.dot(
            jnp.transpose(disp_rows).astype(BF16), tok, preferred_element_type=F32
        )
    mine_ref[...] = rows[:128].astype(BF16)
    other_ref[...] = rows[128:].astype(BF16)


def front(tokens, router):
    return pl.pallas_call(
        front_kernel,
        out_shape=(
            jax.ShapeDtypeStruct((128, D), BF16),
            jax.ShapeDtypeStruct((128, D), BF16),
            jax.ShapeDtypeStruct((2, TOK, ROWS), BF16),
        ),
        in_specs=[pl.BlockSpec(memory_space=pltpu.VMEM)] * 2,
        out_specs=(pl.BlockSpec(memory_space=pltpu.VMEM),) * 3,
        compiler_params=pltpu.CompilerParams(vmem_limit_bytes=20 * 2**20),
        cost_estimate=pl.CostEstimate(flops=900_000_000, bytes_accessed=3_000_000, transcendentals=131072),
    )(tokens, router)


def in_hbm(arrays):
    return [pltpu.with_memory_space_constraint(a, pltpu.HBM) for a in arrays]


def pack_kernel(plans, *refs):
    weights, outs, (buf, in_sem, out_sem) = refs[:3], refs[3 : 3 + len(plans)], refs[3 + len(plans) :]
    p, _ = place()
    loads, stores = [], []
    slot = 0
    for (by, which), out in zip(plans, outs):
        there = pl.ds(2 * ((p + by) & 3), 2)
        for n, t in enumerate(which):
            loads.append(pltpu.make_async_copy(weights[t].at[there], buf.at[slot], in_sem.at[slot]))
            stores.append(pltpu.make_async_copy(buf.at[slot], out.at[n], out_sem.at[slot]))
            slot += 1
    for c in loads:
        c.start()
    for load, store in zip(loads, stores):
        load.wait()
        store.start()
    for c in stores:
        c.wait()


def pack(weights, plans):
    slots = sum(len(which) for _, which in plans)
    return pl.pallas_call(
        functools.partial(pack_kernel, plans),
        out_shape=tuple(jax.ShapeDtypeStruct((len(which), 2, HS, D), BF16) for _, which in plans),
        in_specs=[pl.BlockSpec(memory_space=pl.ANY)] * 3,
        out_specs=(pl.BlockSpec(memory_space=pl.ANY),) * len(plans),
        scratch_shapes=[
            pltpu.VMEM((slots, 2, HS, D), BF16),
            pltpu.SemaphoreType.DMA((slots,)),
            pltpu.SemaphoreType.DMA((slots,)),
        ],
        compiler_params=pltpu.CompilerParams(vmem_limit_bytes=16 * 2**20),
        cost_estimate=pl.CostEstimate(flops=0, bytes_accessed=slots * 1_640_000, transcendentals=0),
    )(*in_hbm(weights))


def reorder_kernel(source, count, *refs):
    parts, outs = refs[:count], refs[count:]
    rows = jnp.concatenate([r[...].reshape(-1, D) for r in parts], axis=0)
    moved = lax.dot_general(
        one_hot(source(columns(ROWS)), ROWS),
        rows,
        (((0,), (0,)), ((), ())),
        preferred_element_type=F32,
    ).astype(BF16)
    start = 0
    for out in outs:
        size = math.prod(out.shape[:-1])
        out[...] = moved[start : start + size].reshape(out.shape)
        start += size


def reorder(parts, source, shapes):
    return pl.pallas_call(
        functools.partial(reorder_kernel, source, len(parts)),
        out_shape=tuple(jax.ShapeDtypeStruct(shape, BF16) for shape in shapes),
        in_specs=[pl.BlockSpec(memory_space=pltpu.VMEM)] * len(parts),
        out_specs=(pl.BlockSpec(memory_space=pltpu.VMEM),) * len(shapes),
        compiler_params=pltpu.CompilerParams(vmem_limit_bytes=16 * 2**20),
        cost_estimate=pl.CostEstimate(flops=170_000_000, bytes_accessed=1_300_000, transcendentals=0),
    )(*parts)


def weave(n):
    return ((n >> 2) & 1) * 128 + (n >> 3) * 4 + (n & 3)


def unweave(n):
    return ((n >> 2) & 31) * 8 + (n >> 7) * 4 + (n & 3)


def deal(n):
    return ((n >> 2) & 31) * 8 + ((n >> 1) & 1) * 4 + (n >> 7) * 2 + (n & 1)


def undeal(n):
    return ((n >> 1) & 1) * 128 + (n >> 3) * 4 + ((n >> 2) & 1) * 2 + (n & 1)


def collect_kernel(*refs):
    weights, moved, (out, sems) = refs[:-5], refs[-5:-2], refs[-2:]
    p, _ = place()
    copies = []
    for j in range(2):
        for t, w in enumerate(weights):
            sources = [w.at[2 * p + j]] + [m.at[t, j] for m in moved]
            for k, src in enumerate(sources):
                dst = out.at[j, pl.ds((4 * t + k) * HS, HS)]
                copies.append(pltpu.make_async_copy(src, dst, sems.at[j, t, k]))
    for c in copies:
        c.start()
    for c in copies:
        c.wait()


def collect(weights, moved):
    count = len(weights)
    return pl.pallas_call(
        collect_kernel,
        out_shape=jax.ShapeDtypeStruct((2, count * 4 * HS, D), BF16),
        in_specs=[pl.BlockSpec(memory_space=pl.ANY)] * (count + 3),
        out_specs=pl.BlockSpec(memory_space=pltpu.VMEM),
        scratch_shapes=[pltpu.SemaphoreType.DMA((2, count, 4))],
        compiler_params=pltpu.CompilerParams(vmem_limit_bytes=16 * 2**20),
        cost_estimate=pl.CostEstimate(flops=0, bytes_accessed=count * 6_600_000, transcendentals=0),
    )(*in_hbm(weights), *moved)


def run_expert(rows, gu, down):
    gu = lax.dot_general(rows, gu, (((1,), (1,)), ((), ())), preferred_element_type=F32)
    gate, up = gu[:, : 4 * HS], gu[:, 4 * HS :]
    act = (gate / (1.0 + jnp.exp(-gate)) * up).astype(BF16)
    return jnp.dot(act, down(), preferred_element_type=F32).astype(BF16)


def experts_kernel(count, *refs):
    slots, (gu_ref, wd_ref, out) = refs[:count], refs[count:]
    for j in range(2):
        rows = jnp.concatenate([s[j] for s in slots], axis=0)
        out[j] = run_expert(rows, gu_ref[j], lambda j=j: wd_ref[j])


def experts(slots, gu, down):
    return pl.pallas_call(
        functools.partial(experts_kernel, len(slots)),
        out_shape=jax.ShapeDtypeStruct((2, 128, D), BF16),
        in_specs=[pl.BlockSpec(memory_space=pltpu.VMEM)] * (len(slots) + 2),
        out_specs=pl.BlockSpec(memory_space=pltpu.VMEM),
        compiler_params=pltpu.CompilerParams(vmem_limit_bytes=24 * 2**20),
        cost_estimate=pl.CostEstimate(
            flops=1_260_000_000, bytes_accessed=2_000_000, transcendentals=327680
        ),
    )(*slots, gu, down)


def first_kernel(sa, sb, gu_ref, wd, d1, d2, d3, oa, ob, down_ref, sems):
    p, _ = place()
    copies = []
    for j in range(2):
        for k, src in enumerate((wd.at[2 * p + j], d1.at[0, j], d2.at[0, j], d3.at[0, j])):
            dst = down_ref.at[j, pl.ds(k * HS, HS)]
            copies.append(pltpu.make_async_copy(src, dst, sems.at[j, k]))
    for c in copies:
        c.start()

    for j in range(2):

        def down(j=j):
            for c in copies[4 * j : 4 * (j + 1)]:
                c.wait()
            return down_ref[j]

        out = run_expert(jnp.concatenate([sa[j], sb[j]], axis=0), gu_ref[j], down)
        oa[j] = out[:128]
        ob[j] = out[128:]


def first_experts(slots, gu, w_down, downs):
    out = jax.ShapeDtypeStruct((2, 128, D), BF16)
    vmem, anywhere = pl.BlockSpec(memory_space=pltpu.VMEM), pl.BlockSpec(memory_space=pl.ANY)
    return pl.pallas_call(
        first_kernel,
        out_shape=(out, out, jax.ShapeDtypeStruct((2, 4 * HS, D), BF16)),
        in_specs=[vmem] * 3 + [anywhere] * 4,
        out_specs=(vmem,) * 3,
        scratch_shapes=[pltpu.SemaphoreType.DMA((2, 4))],
        compiler_params=pltpu.CompilerParams(vmem_limit_bytes=24 * 2**20),
        cost_estimate=pl.CostEstimate(
            flops=2_520_000_000, bytes_accessed=9_000_000, transcendentals=655360
        ),
    )(*slots, gu, *in_hbm((w_down,)), *downs)


def body(tokens, router, w_gate, w_up, w_down):
    ups = pack((w_gate, w_up, w_down), tuple((by, (0, 1)) for by in (1, 2, 3)))
    tokens, router, *ups = lax.optimization_barrier((tokens, router, *ups))
    mine, other, comb = front(tokens, router)
    ups = [shift(w, True, by) for w, by in zip(ups, (1, 2, 3))]
    downs = pack((w_gate, w_up, w_down), tuple((by, (2,)) for by in (1, 2, 3)))
    downs = [shift(w, True, by) for w, by in zip(downs, (1, 2, 3))]
    (rows,) = reorder((mine, swap(other)), weave, ((ROWS, D),))
    rows = exchange(rows)
    rows, *ups = lax.optimization_barrier((rows, *ups))
    (s0,) = reorder((rows,), deal, ((2, 128, D),))
    s1, s3 = shift(s0, False, 1), shift(s0, False, 3)
    gu = collect((w_gate, w_up), ups)
    s1, s3, gu = lax.optimization_barrier((s1, s3, gu))
    far = shift(s1[:, :64], False, 1), shift(s3[:, 64:], False, 3)
    o1, o3, down = first_experts((s1, s3), gu, w_down, downs)
    t1, t3 = shift(o1, False, 3), shift(o3, False, 1)
    *far, _, _ = lax.optimization_barrier((*far, o1, o3))
    o2 = experts(far, gu, down)
    t2 = shift(o2, False, 2)
    s0, _, _ = lax.optimization_barrier((s0, t1, t3))
    o0 = experts((s0,), gu, down)
    total = o0.astype(F32) + t1.astype(F32) + t2.astype(F32) + t3.astype(F32)
    (rows,) = reorder((total.astype(BF16),), undeal, ((ROWS, D),))
    mine, other = reorder((exchange(rows),), unweave, ((128, D),) * 2)
    rows = jnp.concatenate([mine, swap(other)], axis=0)
    mixed = jnp.dot(comb.reshape(2 * TOK, ROWS), rows, preferred_element_type=F32)
    return mixed.astype(BF16).reshape(2, TOK, D)


def solution(mesh):
    return jax.shard_map(
        body,
        mesh=mesh,
        in_specs=(
            P(("dp", "expert"), None, None),
            P(),
            P("expert", "dp", None),
            P("expert", "dp", None),
            P("expert", "dp", None),
        ),
        out_specs=P(("dp", "expert"), None, None),
        check_vma=False,
    )
```

```python
import functools
import math

import jax
import jax.numpy as jnp
from jax import lax
from jax.experimental import pallas as pl
from jax.experimental.pallas import tpu as pltpu
from jax.sharding import PartitionSpec as P

D = 1280
EXPERTS = 128
TOK = 256
HS = 160
ROWS = 256
AXES = ("dp", "expert")
F32 = jnp.float32
BF16 = jnp.bfloat16


def place():
    dp = lax.axis_index("dp")
    core = lax.axis_index("expert") & 1
    y, x = dp >> 2, dp & 3
    p = jnp.where(core == 0, x, y)
    q = jnp.where(core == 0, y, x)
    return p, q


def shift_pairs(along_p, by):
    pairs = []
    for y in range(4):
        for x in range(4):
            for e in range(16):
                move_x = (e % 2 == 0) == along_p
                ny, nx = (y, (x + by) % 4) if move_x else ((y + by) % 4, x)
                pairs.append(((y * 4 + x) * 16 + e, (ny * 4 + nx) * 16 + e))
    return pairs


GROUPS = [
    [
        ((f * 4 + p) if core == 0 else (p * 4 + f)) * 16 + z * 2 + core
        for p in range(4)
        for z in range(8)
    ]
    for core in range(2)
    for f in range(4)
]


def exchange(rows):
    return lax.all_to_all(
        rows, AXES, split_axis=0, concat_axis=0, tiled=True, axis_index_groups=GROUPS
    )


def swap(value):
    return lax.ppermute(value, "expert", [(e, e ^ 1) for e in range(16)])


def shift(value, along_p, by):
    return lax.ppermute(value, AXES, shift_pairs(along_p, by))


def one_hot(chosen, lines):
    line = lax.broadcasted_iota(jnp.int32, (lines, ROWS), 0)
    return jnp.where(chosen == line, 1.0, 0.0).astype(BF16)


def columns(lines):
    return lax.broadcasted_iota(jnp.int32, (lines, ROWS), 1)


def front_kernel(tok_ref, router_ref, mine_ref, other_ref, comb_ref):
    row = columns(EXPERTS)
    core = (lax.axis_index("expert") & 1) ^ (row >> 7)
    expert = ((row >> 2) & 7) * 16 + core * 8 + ((row >> 5) & 3) * 2 + ((row >> 1) & 1)
    r = router_ref[...]
    r0 = r.astype(BF16)
    rest = r - r0.astype(F32)
    r1 = rest.astype(BF16)
    r2 = (rest - r1.astype(F32)).astype(BF16)
    rows = jnp.zeros((ROWS, D), F32)
    for i in range(2):
        tok = tok_ref[i]
        logits = (
            jnp.dot(tok, r2, preferred_element_type=F32)
            + jnp.dot(tok, r1, preferred_element_type=F32)
            + jnp.dot(tok, r0, preferred_element_type=F32)
        )
        select = one_hot(jnp.where((row & 1) == i, expert, -1), EXPERTS)
        ex = jnp.exp(logits - jnp.max(logits, axis=0, keepdims=True))
        disp = (ex / jnp.sum(ex, axis=0, keepdims=True)).astype(BF16)
        ec = jnp.exp(logits - jnp.max(logits, axis=1, keepdims=True))
        comb = (ec / jnp.sum(ec, axis=1, keepdims=True)).astype(BF16)
        disp_rows = jnp.dot(disp, select, preferred_element_type=F32)
        comb_ref[i] = jnp.dot(comb, select, preferred_element_type=F32).astype(BF16)
        rows = rows + jnp.dot(
            jnp.transpose(disp_rows).astype(BF16), tok, preferred_element_type=F32
        )
    mine_ref[...] = rows[:128].astype(BF16)
    other_ref[...] = rows[128:].astype(BF16)


def front(tokens, router):
    return pl.pallas_call(
        front_kernel,
        out_shape=(
            jax.ShapeDtypeStruct((128, D), BF16),
            jax.ShapeDtypeStruct((128, D), BF16),
            jax.ShapeDtypeStruct((2, TOK, ROWS), BF16),
        ),
        in_specs=[pl.BlockSpec(memory_space=pltpu.VMEM)] * 2,
        out_specs=(pl.BlockSpec(memory_space=pltpu.VMEM),) * 3,
        compiler_params=pltpu.CompilerParams(vmem_limit_bytes=20 * 2**20),
        cost_estimate=pl.CostEstimate(flops=900_000_000, bytes_accessed=3_000_000, transcendentals=131072),
    )(tokens, router)


def in_hbm(arrays):
    return [pltpu.with_memory_space_constraint(a, pltpu.HBM) for a in arrays]


def pack_kernel(plans, *refs):
    weights, outs, (buf, in_sem, out_sem) = refs[:3], refs[3 : 3 + len(plans)], refs[3 + len(plans) :]
    p, _ = place()
    loads, stores = [], []
    slot = 0
    for (by, which), out in zip(plans, outs):
        there = pl.ds(2 * ((p + by) & 3), 2)
        for n, t in enumerate(which):
            loads.append(pltpu.make_async_copy(weights[t].at[there], buf.at[slot], in_sem.at[slot]))
            stores.append(pltpu.make_async_copy(buf.at[slot], out.at[n], out_sem.at[slot]))
            slot += 1
    for c in loads:
        c.start()
    for load, store in zip(loads, stores):
        load.wait()
        store.start()
    for c in stores:
        c.wait()


def pack(weights, plans):
    slots = sum(len(which) for _, which in plans)
    return pl.pallas_call(
        functools.partial(pack_kernel, plans),
        out_shape=tuple(jax.ShapeDtypeStruct((len(which), 2, HS, D), BF16) for _, which in plans),
        in_specs=[pl.BlockSpec(memory_space=pl.ANY)] * 3,
        out_specs=(pl.BlockSpec(memory_space=pl.ANY),) * len(plans),
        scratch_shapes=[
            pltpu.VMEM((slots, 2, HS, D), BF16),
            pltpu.SemaphoreType.DMA((slots,)),
            pltpu.SemaphoreType.DMA((slots,)),
        ],
        compiler_params=pltpu.CompilerParams(vmem_limit_bytes=16 * 2**20),
        cost_estimate=pl.CostEstimate(flops=0, bytes_accessed=slots * 1_640_000, transcendentals=0),
    )(*in_hbm(weights))


def reorder_kernel(source, count, added, *refs):
    parts, terms, outs = refs[:count], refs[count : count + added], refs[count + added :]
    rows = jnp.concatenate([r[...].reshape(-1, D) for r in parts], axis=0)
    if terms:
        rows = rows.astype(F32)
        for t in terms:
            rows = rows + t[...].reshape(-1, D).astype(F32)
        rows = rows.astype(BF16)
    moved = lax.dot_general(
        one_hot(source(columns(ROWS)), ROWS),
        rows,
        (((0,), (0,)), ((), ())),
        preferred_element_type=F32,
    ).astype(BF16)
    start = 0
    for out in outs:
        size = math.prod(out.shape[:-1])
        out[...] = moved[start : start + size].reshape(out.shape)
        start += size


def reorder(parts, source, shapes, terms=()):
    return pl.pallas_call(
        functools.partial(reorder_kernel, source, len(parts), len(terms)),
        out_shape=tuple(jax.ShapeDtypeStruct(shape, BF16) for shape in shapes),
        in_specs=[pl.BlockSpec(memory_space=pltpu.VMEM)] * (len(parts) + len(terms)),
        out_specs=(pl.BlockSpec(memory_space=pltpu.VMEM),) * len(shapes),
        compiler_params=pltpu.CompilerParams(vmem_limit_bytes=16 * 2**20),
        cost_estimate=pl.CostEstimate(flops=170_000_000, bytes_accessed=1_300_000, transcendentals=0),
    )(*parts, *terms)


def weave(n):
    return ((n >> 2) & 1) * 128 + (n >> 3) * 4 + (n & 3)


def unweave(n):
    return ((n >> 2) & 31) * 8 + (n >> 7) * 4 + (n & 3)


def deal(n):
    return ((n >> 2) & 31) * 8 + ((n >> 1) & 1) * 4 + (n >> 7) * 2 + (n & 1)


def undeal(n):
    return ((n >> 1) & 1) * 128 + (n >> 3) * 4 + ((n >> 2) & 1) * 2 + (n & 1)


def collect_kernel(*refs):
    weights, moved, (out, sems) = refs[:-5], refs[-5:-2], refs[-2:]
    p, _ = place()
    copies = []
    for j in range(2):
        for t, w in enumerate(weights):
            sources = [w.at[2 * p + j]] + [m.at[t, j] for m in moved]
            for k, src in enumerate(sources):
                dst = out.at[j, pl.ds((4 * t + k) * HS, HS)]
                copies.append(pltpu.make_async_copy(src, dst, sems.at[j, t, k]))
    for c in copies:
        c.start()
    for c in copies:
        c.wait()


def collect(weights, moved):
    count = len(weights)
    return pl.pallas_call(
        collect_kernel,
        out_shape=jax.ShapeDtypeStruct((2, count * 4 * HS, D), BF16),
        in_specs=[pl.BlockSpec(memory_space=pl.ANY)] * (count + 3),
        out_specs=pl.BlockSpec(memory_space=pltpu.VMEM),
        scratch_shapes=[pltpu.SemaphoreType.DMA((2, count, 4))],
        compiler_params=pltpu.CompilerParams(vmem_limit_bytes=16 * 2**20),
        cost_estimate=pl.CostEstimate(flops=0, bytes_accessed=count * 6_600_000, transcendentals=0),
    )(*in_hbm(weights), *moved)


def run_expert(rows, gu, down):
    gu = lax.dot_general(rows, gu, (((1,), (1,)), ((), ())), preferred_element_type=F32)
    gate, up = gu[:, : 4 * HS], gu[:, 4 * HS :]
    act = (gate / (1.0 + jnp.exp(-gate)) * up).astype(BF16)
    return jnp.dot(act, down(), preferred_element_type=F32).astype(BF16)


def experts_kernel(far_low, far_high, own, gu_ref, wd_ref, far_out, own_out):
    for j in range(2):
        rows = jnp.concatenate([far_low[j], far_high[j], own[j]], axis=0)
        out = run_expert(rows, gu_ref[j], lambda j=j: wd_ref[j])
        far_out[j] = out[:128]
        own_out[j] = out[128:]


def experts(slots, gu, down):
    return pl.pallas_call(
        experts_kernel,
        out_shape=(jax.ShapeDtypeStruct((2, 128, D), BF16),) * 2,
        in_specs=[pl.BlockSpec(memory_space=pltpu.VMEM)] * 5,
        out_specs=(pl.BlockSpec(memory_space=pltpu.VMEM),) * 2,
        compiler_params=pltpu.CompilerParams(vmem_limit_bytes=24 * 2**20),
        cost_estimate=pl.CostEstimate(
            flops=1_260_000_000, bytes_accessed=2_000_000, transcendentals=327680
        ),
    )(*slots, gu, down)


def add_kernel(a, b, c, out):
    out[...] = a[...].astype(F32) + b[...].astype(F32) + c[...].astype(F32)


def add(a, b, c):
    return pl.pallas_call(
        add_kernel,
        out_shape=jax.ShapeDtypeStruct(a.shape, F32),
        in_specs=[pl.BlockSpec(memory_space=pltpu.VMEM)] * 3,
        out_specs=pl.BlockSpec(memory_space=pltpu.VMEM),
        compiler_params=pltpu.CompilerParams(vmem_limit_bytes=16 * 2**20),
        cost_estimate=pl.CostEstimate(flops=1_260_000_000, bytes_accessed=3_300_000, transcendentals=0),
    )(a, b, c)


def first_kernel(sa, sb, gu_ref, wd, d1, d2, d3, oa, ob, down_ref, sems):
    p, _ = place()
    copies = []
    for j in range(2):
        for k, src in enumerate((wd.at[2 * p + j], d1.at[0, j], d2.at[0, j], d3.at[0, j])):
            dst = down_ref.at[j, pl.ds(k * HS, HS)]
            copies.append(pltpu.make_async_copy(src, dst, sems.at[j, k]))
    for c in copies:
        c.start()

    for j in range(2):

        def down(j=j):
            for c in copies[4 * j : 4 * (j + 1)]:
                c.wait()
            return down_ref[j]

        out = run_expert(jnp.concatenate([sa[j], sb[j]], axis=0), gu_ref[j], down)
        oa[j] = out[:128]
        ob[j] = out[128:]


def first_experts(slots, gu, w_down, downs):
    out = jax.ShapeDtypeStruct((2, 128, D), BF16)
    vmem, anywhere = pl.BlockSpec(memory_space=pltpu.VMEM), pl.BlockSpec(memory_space=pl.ANY)
    return pl.pallas_call(
        first_kernel,
        out_shape=(out, out, jax.ShapeDtypeStruct((2, 4 * HS, D), BF16)),
        in_specs=[vmem] * 3 + [anywhere] * 4,
        out_specs=(vmem,) * 3,
        scratch_shapes=[pltpu.SemaphoreType.DMA((2, 4))],
        compiler_params=pltpu.CompilerParams(vmem_limit_bytes=24 * 2**20),
        cost_estimate=pl.CostEstimate(
            flops=2_520_000_000, bytes_accessed=9_000_000, transcendentals=655360
        ),
    )(*slots, gu, *in_hbm((w_down,)), *downs)


def body(tokens, router, w_gate, w_up, w_down):
    ups = pack((w_gate, w_up, w_down), tuple((by, (0, 1)) for by in (1, 2, 3)))
    tokens, router, *ups = lax.optimization_barrier((tokens, router, *ups))
    mine, other, comb = front(tokens, router)
    ups = [shift(w, True, by) for w, by in zip(ups, (1, 2, 3))]
    downs = pack((w_gate, w_up, w_down), tuple((by, (2,)) for by in (1, 2, 3)))
    downs = [shift(w, True, by) for w, by in zip(downs, (1, 2, 3))]
    (rows,) = reorder((mine, swap(other)), weave, ((ROWS, D),))
    rows = exchange(rows)
    rows, *ups = lax.optimization_barrier((rows, *ups))
    (s0,) = reorder((rows,), deal, ((2, 128, D),))
    s1, s3 = shift(s0, False, 1), shift(s0, False, 3)
    gu = collect((w_gate, w_up), ups)
    s1, s3, gu = lax.optimization_barrier((s1, s3, gu))
    far = shift(s1[:, :64], False, 1), shift(s3[:, 64:], False, 3)
    o1, o3, down = first_experts((s1, s3), gu, w_down, downs)
    t1, t3 = shift(o1, False, 3), shift(o3, False, 1)
    *far, _, _ = lax.optimization_barrier((*far, o1, o3))
    o2, o0 = experts((*far, s0), gu, down)
    t2 = shift(o2, False, 2)
    partial = add(o0, t1, t3)
    (rows,) = reorder((partial,), undeal, ((ROWS, D),), (t2,))
    mine, other = reorder((exchange(rows),), unweave, ((128, D),) * 2)
    rows = jnp.concatenate([mine, swap(other)], axis=0)
    mixed = jnp.dot(comb.reshape(2 * TOK, ROWS), rows, preferred_element_type=F32)
    return mixed.astype(BF16).reshape(2, TOK, D)


def solution(mesh):
    return jax.shard_map(
        body,
        mesh=mesh,
        in_specs=(
            P(("dp", "expert"), None, None),
            P(),
            P("expert", "dp", None),
            P("expert", "dp", None),
            P("expert", "dp", None),
        ),
        out_specs=P(("dp", "expert"), None, None),
        check_vma=False,
    )
```

```python
import functools
import math

import jax
import jax.numpy as jnp
from jax import lax
from jax.experimental import pallas as pl
from jax.experimental.pallas import tpu as pltpu
from jax.sharding import PartitionSpec as P

D = 1280
EXPERTS = 128
TOK = 256
HS = 160
ROWS = 256
AXES = ("dp", "expert")
F32 = jnp.float32
BF16 = jnp.bfloat16


def place():
    dp = lax.axis_index("dp")
    core = lax.axis_index("expert") & 1
    y, x = dp >> 2, dp & 3
    p = jnp.where(core == 0, x, y)
    q = jnp.where(core == 0, y, x)
    return p, q


def shift_pairs(along_p, by):
    pairs = []
    for y in range(4):
        for x in range(4):
            for e in range(16):
                move_x = (e % 2 == 0) == along_p
                ny, nx = (y, (x + by) % 4) if move_x else ((y + by) % 4, x)
                pairs.append(((y * 4 + x) * 16 + e, (ny * 4 + nx) * 16 + e))
    return pairs


GROUPS = [
    [
        ((f * 4 + p) if core == 0 else (p * 4 + f)) * 16 + z * 2 + core
        for p in range(4)
        for z in range(8)
    ]
    for core in range(2)
    for f in range(4)
]


def exchange(rows):
    return lax.all_to_all(
        rows, AXES, split_axis=0, concat_axis=0, tiled=True, axis_index_groups=GROUPS
    )


def swap(value):
    return lax.ppermute(value, "expert", [(e, e ^ 1) for e in range(16)])


def shift(value, along_p, by):
    return lax.ppermute(value, AXES, shift_pairs(along_p, by))


def one_hot(chosen, lines):
    line = lax.broadcasted_iota(jnp.int32, (lines, ROWS), 0)
    return jnp.where(chosen == line, 1.0, 0.0).astype(BF16)


def columns(lines):
    return lax.broadcasted_iota(jnp.int32, (lines, ROWS), 1)


def front_kernel(tok_ref, router_ref, mine_ref, other_ref, comb_ref):
    row = columns(EXPERTS)
    core = (lax.axis_index("expert") & 1) ^ (row >> 7)
    expert = ((row >> 2) & 7) * 16 + core * 8 + ((row >> 5) & 3) * 2 + ((row >> 1) & 1)
    r = router_ref[...]
    r0 = r.astype(BF16)
    rest = r - r0.astype(F32)
    r1 = rest.astype(BF16)
    r2 = (rest - r1.astype(F32)).astype(BF16)
    rows = jnp.zeros((ROWS, D), F32)
    for i in range(2):
        tok = tok_ref[i]
        logits = (
            jnp.dot(tok, r2, preferred_element_type=F32)
            + jnp.dot(tok, r1, preferred_element_type=F32)
            + jnp.dot(tok, r0, preferred_element_type=F32)
        )
        select = one_hot(jnp.where((row & 1) == i, expert, -1), EXPERTS)
        ex = jnp.exp(logits - jnp.max(logits, axis=0, keepdims=True))
        disp = (ex / jnp.sum(ex, axis=0, keepdims=True)).astype(BF16)
        ec = jnp.exp(logits - jnp.max(logits, axis=1, keepdims=True))
        comb = (ec / jnp.sum(ec, axis=1, keepdims=True)).astype(BF16)
        disp_rows = jnp.dot(disp, select, preferred_element_type=F32)
        comb_ref[i] = jnp.dot(comb, select, preferred_element_type=F32).astype(BF16)
        rows = rows + jnp.dot(
            jnp.transpose(disp_rows).astype(BF16), tok, preferred_element_type=F32
        )
    mine_ref[...] = rows[:128].astype(BF16)
    other_ref[...] = rows[128:].astype(BF16)


def front(tokens, router):
    return pl.pallas_call(
        front_kernel,
        out_shape=(
            jax.ShapeDtypeStruct((128, D), BF16),
            jax.ShapeDtypeStruct((128, D), BF16),
            jax.ShapeDtypeStruct((2, TOK, ROWS), BF16),
        ),
        in_specs=[pl.BlockSpec(memory_space=pltpu.VMEM)] * 2,
        out_specs=(pl.BlockSpec(memory_space=pltpu.VMEM),) * 3,
        compiler_params=pltpu.CompilerParams(vmem_limit_bytes=20 * 2**20),
        cost_estimate=pl.CostEstimate(flops=900_000_000, bytes_accessed=3_000_000, transcendentals=131072),
    )(tokens, router)


def in_hbm(arrays):
    return [pltpu.with_memory_space_constraint(a, pltpu.HBM) for a in arrays]


def pack_kernel(plans, *refs):
    weights, outs, (buf, in_sem, out_sem) = refs[:3], refs[3 : 3 + len(plans)], refs[3 + len(plans) :]
    p, _ = place()
    loads, stores = [], []
    slot = 0
    for (by, which), out in zip(plans, outs):
        there = pl.ds(2 * ((p + by) & 3), 2)
        for n, t in enumerate(which):
            loads.append(pltpu.make_async_copy(weights[t].at[there], buf.at[slot], in_sem.at[slot]))
            stores.append(pltpu.make_async_copy(buf.at[slot], out.at[n], out_sem.at[slot]))
            slot += 1
    for c in loads:
        c.start()
    for load, store in zip(loads, stores):
        load.wait()
        store.start()
    for c in stores:
        c.wait()


def pack(weights, plans):
    slots = sum(len(which) for _, which in plans)
    return pl.pallas_call(
        functools.partial(pack_kernel, plans),
        out_shape=tuple(jax.ShapeDtypeStruct((len(which), 2, HS, D), BF16) for _, which in plans),
        in_specs=[pl.BlockSpec(memory_space=pl.ANY)] * 3,
        out_specs=(pl.BlockSpec(memory_space=pl.ANY),) * len(plans),
        scratch_shapes=[
            pltpu.VMEM((slots, 2, HS, D), BF16),
            pltpu.SemaphoreType.DMA((slots,)),
            pltpu.SemaphoreType.DMA((slots,)),
        ],
        compiler_params=pltpu.CompilerParams(vmem_limit_bytes=16 * 2**20),
        cost_estimate=pl.CostEstimate(flops=0, bytes_accessed=slots * 1_640_000, transcendentals=0),
    )(*in_hbm(weights))


def reorder_kernel(source, count, added, *refs):
    parts, terms, outs = refs[:count], refs[count : count + added], refs[count + added :]
    rows = jnp.concatenate([r[...].reshape(-1, D) for r in parts], axis=0)
    if terms:
        rows = rows.astype(F32)
        for t in terms:
            rows = rows + t[...].reshape(-1, D).astype(F32)
        rows = rows.astype(BF16)
    moved = lax.dot_general(
        one_hot(source(columns(ROWS)), ROWS),
        rows,
        (((0,), (0,)), ((), ())),
        preferred_element_type=F32,
    ).astype(BF16)
    start = 0
    for out in outs:
        size = math.prod(out.shape[:-1])
        out[...] = moved[start : start + size].reshape(out.shape)
        start += size


def reorder(parts, source, shapes, terms=()):
    return pl.pallas_call(
        functools.partial(reorder_kernel, source, len(parts), len(terms)),
        out_shape=tuple(jax.ShapeDtypeStruct(shape, BF16) for shape in shapes),
        in_specs=[pl.BlockSpec(memory_space=pltpu.VMEM)] * (len(parts) + len(terms)),
        out_specs=(pl.BlockSpec(memory_space=pltpu.VMEM),) * len(shapes),
        compiler_params=pltpu.CompilerParams(vmem_limit_bytes=16 * 2**20),
        cost_estimate=pl.CostEstimate(flops=170_000_000, bytes_accessed=1_300_000, transcendentals=0),
    )(*parts, *terms)


def weave(n):
    return ((n >> 2) & 1) * 128 + (n >> 3) * 4 + (n & 3)


def unweave(n):
    return ((n >> 2) & 31) * 8 + (n >> 7) * 4 + (n & 3)


def deal(n):
    return ((n >> 2) & 31) * 8 + ((n >> 1) & 1) * 4 + (n >> 7) * 2 + (n & 1)


def undeal(n):
    return ((n >> 1) & 1) * 128 + (n >> 3) * 4 + ((n >> 2) & 1) * 2 + (n & 1)


def collect_kernel(*refs):
    weights, moved, (out, sems) = refs[:-5], refs[-5:-2], refs[-2:]
    p, _ = place()
    copies = []
    for j in range(2):
        for t, w in enumerate(weights):
            sources = [w.at[2 * p + j]] + [m.at[t, j] for m in moved]
            for k, src in enumerate(sources):
                dst = out.at[j, pl.ds((4 * t + k) * HS, HS)]
                copies.append(pltpu.make_async_copy(src, dst, sems.at[j, t, k]))
    for c in copies:
        c.start()
    for c in copies:
        c.wait()


def collect(weights, moved):
    count = len(weights)
    return pl.pallas_call(
        collect_kernel,
        out_shape=jax.ShapeDtypeStruct((2, count * 4 * HS, D), BF16),
        in_specs=[pl.BlockSpec(memory_space=pl.ANY)] * (count + 3),
        out_specs=pl.BlockSpec(memory_space=pltpu.VMEM),
        scratch_shapes=[pltpu.SemaphoreType.DMA((2, count, 4))],
        compiler_params=pltpu.CompilerParams(vmem_limit_bytes=16 * 2**20),
        cost_estimate=pl.CostEstimate(flops=0, bytes_accessed=count * 6_600_000, transcendentals=0),
    )(*in_hbm(weights), *moved)


def run_up(rows, gu):
    gu = lax.dot_general(rows, gu, (((1,), (1,)), ((), ())), preferred_element_type=F32)
    gate, up = gu[:, : 4 * HS], gu[:, 4 * HS :]
    return (gate / (1.0 + jnp.exp(-gate)) * up).astype(BF16)


def experts_kernel(far_low, far_high, own, gu_ref, wd_ref, far_out, own_out):
    for j in range(2):
        rows = jnp.concatenate([far_low[j], far_high[j], own[j]], axis=0)
        act = run_up(rows, gu_ref[j])
        out = jnp.dot(act, wd_ref[j], preferred_element_type=F32).astype(BF16)
        far_out[j] = out[:128]
        own_out[j] = out[128:]


def experts(slots, gu, down):
    return pl.pallas_call(
        experts_kernel,
        out_shape=(jax.ShapeDtypeStruct((2, 128, D), BF16),) * 2,
        in_specs=[pl.BlockSpec(memory_space=pltpu.VMEM)] * 5,
        out_specs=(pl.BlockSpec(memory_space=pltpu.VMEM),) * 2,
        compiler_params=pltpu.CompilerParams(vmem_limit_bytes=24 * 2**20),
        cost_estimate=pl.CostEstimate(
            flops=1_260_000_000, bytes_accessed=2_000_000, transcendentals=327680
        ),
    )(*slots, gu, down)


def add_kernel(a, b, c, out):
    out[...] = a[...].astype(F32) + b[...].astype(F32) + c[...].astype(F32)


def add(a, b, c):
    return pl.pallas_call(
        add_kernel,
        out_shape=jax.ShapeDtypeStruct(a.shape, F32),
        in_specs=[pl.BlockSpec(memory_space=pltpu.VMEM)] * 3,
        out_specs=pl.BlockSpec(memory_space=pltpu.VMEM),
        compiler_params=pltpu.CompilerParams(vmem_limit_bytes=16 * 2**20),
        cost_estimate=pl.CostEstimate(flops=1_260_000_000, bytes_accessed=3_300_000, transcendentals=0),
    )(a, b, c)


def up_kernel(sa, sb, gu_ref, act_ref):
    for j in range(2):
        act_ref[j] = run_up(jnp.concatenate([sa[j], sb[j]], axis=0), gu_ref[j])


def up_half(sa, sb, gu):
    return pl.pallas_call(
        up_kernel,
        out_shape=jax.ShapeDtypeStruct((2, 256, 4 * HS), BF16),
        in_specs=[pl.BlockSpec(memory_space=pltpu.VMEM)] * 3,
        out_specs=pl.BlockSpec(memory_space=pltpu.VMEM),
        compiler_params=pltpu.CompilerParams(vmem_limit_bytes=16 * 2**20),
        cost_estimate=pl.CostEstimate(
            flops=0, bytes_accessed=0, transcendentals=0
        ),
    )(sa, sb, gu)


def down_kernel(act, wd, d1, d3, d2, oa, ob, down_ref, sems):
    p, _ = place()
    copies = []
    for j in range(2):
        for k, src in enumerate((wd.at[2 * p + j], d1.at[0, j], d2.at[0, j], d3.at[0, j])):
            dst = down_ref.at[j, pl.ds(k * HS, HS)]
            copies.append(pltpu.make_async_copy(src, dst, sems.at[j, k]))
    for c in copies:
        c.start()
    for j in range(2):
        for c in copies[4 * j : 4 * (j + 1)]:
            c.wait()
        out = jnp.dot(act[j], down_ref[j], preferred_element_type=F32).astype(BF16)
        oa[j] = out[:128]
        ob[j] = out[128:]


def down_half(act, w_down, downs):
    out = jax.ShapeDtypeStruct((2, 128, D), BF16)
    vmem, anywhere = pl.BlockSpec(memory_space=pltpu.VMEM), pl.BlockSpec(memory_space=pl.ANY)
    return pl.pallas_call(
        down_kernel,
        out_shape=(out, out, jax.ShapeDtypeStruct((2, 4 * HS, D), BF16)),
        in_specs=[vmem] + [anywhere] * 4,
        out_specs=(vmem,) * 3,
        scratch_shapes=[pltpu.SemaphoreType.DMA((2, 4))],
        compiler_params=pltpu.CompilerParams(vmem_limit_bytes=16 * 2**20),
        cost_estimate=pl.CostEstimate(flops=2_520_000_000, bytes_accessed=9_000_000, transcendentals=655360),
    )(act, *in_hbm((w_down,)), *downs)


def body(tokens, router, w_gate, w_up, w_down):
    ups = pack((w_gate, w_up, w_down), tuple((by, (0, 1)) for by in (2, 1, 3)))
    tokens, router, *ups = lax.optimization_barrier((tokens, router, *ups))
    mine, other, comb = front(tokens, router)
    ups = [shift(w, True, by) for w, by in zip(ups, (2, 1, 3))]
    downs = pack((w_gate, w_up, w_down), tuple((by, (2,)) for by in (1, 2, 3)))
    downs = [shift(w, True, by) for w, by in zip(downs, (1, 2, 3))]
    (rows,) = reorder((mine, swap(other)), weave, ((ROWS, D),))
    rows = exchange(rows)
    rows, *ups = lax.optimization_barrier((rows, *ups))
    ups = [ups[n] for n in (1, 0, 2)]
    (s0,) = reorder((rows,), deal, ((2, 128, D),))
    s1, s3 = shift(s0, False, 1), shift(s0, False, 3)
    gu = collect((w_gate, w_up), ups)
    s1, s3, gu = lax.optimization_barrier((s1, s3, gu))
    far = shift(s1[:, :64], False, 1), shift(s3[:, 64:], False, 3)
    o1, o3, down = down_half(up_half(s1, s3, gu), w_down, (downs[0], downs[2], downs[1]))
    t1, t3 = shift(o1, False, 3), shift(o3, False, 1)
    *far, _, _ = lax.optimization_barrier((*far, o1, o3))
    o2, o0 = experts((*far, s0), gu, down)
    t2 = shift(o2, False, 2)
    partial = add(o0, t1, t3)
    (rows,) = reorder((partial,), undeal, ((ROWS, D),), (t2,))
    mine, other = reorder((exchange(rows),), unweave, ((128, D),) * 2)
    rows = jnp.concatenate([mine, swap(other)], axis=0)
    mixed = jnp.dot(comb.reshape(2 * TOK, ROWS), rows, preferred_element_type=F32)
    return mixed.astype(BF16).reshape(2, TOK, D)


def solution(mesh):
    return jax.shard_map(
        body,
        mesh=mesh,
        in_specs=(
            P(("dp", "expert"), None, None),
            P(),
            P("expert", "dp", None),
            P("expert", "dp", None),
            P("expert", "dp", None),
        ),
        out_specs=P(("dp", "expert"), None, None),
        check_vma=False,
    )
```

```python
import functools
import math

import jax
import jax.numpy as jnp
from jax import lax
from jax.experimental import pallas as pl
from jax.experimental.pallas import tpu as pltpu
from jax.sharding import PartitionSpec as P

D = 1280
EXPERTS = 128
TOK = 256
HS = 160
ROWS = 256
AXES = ("dp", "expert")
F32 = jnp.float32
BF16 = jnp.bfloat16


def place():
    dp = lax.axis_index("dp")
    core = lax.axis_index("expert") & 1
    y, x = dp >> 2, dp & 3
    p = jnp.where(core == 0, x, y)
    q = jnp.where(core == 0, y, x)
    return p, q


def shift_pairs(along_p, by):
    pairs = []
    for y in range(4):
        for x in range(4):
            for e in range(16):
                move_x = (e % 2 == 0) == along_p
                ny, nx = (y, (x + by) % 4) if move_x else ((y + by) % 4, x)
                pairs.append(((y * 4 + x) * 16 + e, (ny * 4 + nx) * 16 + e))
    return pairs


GROUPS = [
    [
        ((f * 4 + p) if core == 0 else (p * 4 + f)) * 16 + z * 2 + core
        for p in range(4)
        for z in range(8)
    ]
    for core in range(2)
    for f in range(4)
]


def exchange(rows):
    return lax.all_to_all(
        rows, AXES, split_axis=0, concat_axis=0, tiled=True, axis_index_groups=GROUPS
    )


def swap(value):
    return lax.ppermute(value, "expert", [(e, e ^ 1) for e in range(16)])


def shift(value, along_p, by):
    return lax.ppermute(value, AXES, shift_pairs(along_p, by))


def one_hot(chosen, lines):
    line = lax.broadcasted_iota(jnp.int32, (lines, ROWS), 0)
    return jnp.where(chosen == line, 1.0, 0.0).astype(BF16)


def columns(lines):
    return lax.broadcasted_iota(jnp.int32, (lines, ROWS), 1)


def front_kernel(tok_ref, router_ref, mine_ref, other_ref, comb_ref):
    row = columns(EXPERTS)
    core = (lax.axis_index("expert") & 1) ^ (row >> 7)
    expert = ((row >> 2) & 7) * 16 + core * 8 + ((row >> 5) & 3) * 2 + ((row >> 1) & 1)
    r = router_ref[...]
    r0 = r.astype(BF16)
    rest = r - r0.astype(F32)
    r1 = rest.astype(BF16)
    r2 = (rest - r1.astype(F32)).astype(BF16)
    rows = jnp.zeros((ROWS, D), F32)
    for i in range(2):
        tok = tok_ref[i]
        logits = (
            jnp.dot(tok, r2, preferred_element_type=F32)
            + jnp.dot(tok, r1, preferred_element_type=F32)
            + jnp.dot(tok, r0, preferred_element_type=F32)
        )
        select = one_hot(jnp.where((row & 1) == i, expert, -1), EXPERTS)
        ex = jnp.exp(logits - jnp.max(logits, axis=0, keepdims=True))
        disp = (ex / jnp.sum(ex, axis=0, keepdims=True)).astype(BF16)
        ec = jnp.exp(logits - jnp.max(logits, axis=1, keepdims=True))
        comb = (ec / jnp.sum(ec, axis=1, keepdims=True)).astype(BF16)
        disp_rows = jnp.dot(disp, select, preferred_element_type=F32)
        comb_ref[i] = jnp.dot(comb, select, preferred_element_type=F32).astype(BF16)
        rows = rows + jnp.dot(
            jnp.transpose(disp_rows).astype(BF16), tok, preferred_element_type=F32
        )
    mine_ref[...] = rows[:128].astype(BF16)
    other_ref[...] = rows[128:].astype(BF16)


def front(tokens, router):
    return pl.pallas_call(
        front_kernel,
        out_shape=(
            jax.ShapeDtypeStruct((128, D), BF16),
            jax.ShapeDtypeStruct((128, D), BF16),
            jax.ShapeDtypeStruct((2, TOK, ROWS), BF16),
        ),
        in_specs=[pl.BlockSpec(memory_space=pltpu.VMEM)] * 2,
        out_specs=(pl.BlockSpec(memory_space=pltpu.VMEM),) * 3,
        compiler_params=pltpu.CompilerParams(vmem_limit_bytes=20 * 2**20),
        cost_estimate=pl.CostEstimate(flops=900_000_000, bytes_accessed=3_000_000, transcendentals=131072),
    )(tokens, router)


def in_hbm(arrays):
    return [pltpu.with_memory_space_constraint(a, pltpu.HBM) for a in arrays]


def pack_kernel(plans, *refs):
    weights, outs, (buf, in_sem, out_sem) = refs[:3], refs[3 : 3 + len(plans)], refs[3 + len(plans) :]
    p, _ = place()
    loads, stores = [], []
    slot = 0
    for (by, which), out in zip(plans, outs):
        there = pl.ds(2 * ((p + by) & 3), 2)
        for n, t in enumerate(which):
            loads.append(pltpu.make_async_copy(weights[t].at[there], buf.at[slot], in_sem.at[slot]))
            stores.append(pltpu.make_async_copy(buf.at[slot], out.at[n], out_sem.at[slot]))
            slot += 1
    for c in loads:
        c.start()
    for load, store in zip(loads, stores):
        load.wait()
        store.start()
    for c in stores:
        c.wait()


def pack(weights, plans):
    slots = sum(len(which) for _, which in plans)
    return pl.pallas_call(
        functools.partial(pack_kernel, plans),
        out_shape=tuple(jax.ShapeDtypeStruct((len(which), 2, HS, D), BF16) for _, which in plans),
        in_specs=[pl.BlockSpec(memory_space=pl.ANY)] * 3,
        out_specs=(pl.BlockSpec(memory_space=pl.ANY),) * len(plans),
        scratch_shapes=[
            pltpu.VMEM((slots, 2, HS, D), BF16),
            pltpu.SemaphoreType.DMA((slots,)),
            pltpu.SemaphoreType.DMA((slots,)),
        ],
        compiler_params=pltpu.CompilerParams(vmem_limit_bytes=16 * 2**20),
        cost_estimate=pl.CostEstimate(flops=0, bytes_accessed=slots * 1_640_000, transcendentals=0),
    )(*in_hbm(weights))


def reorder_kernel(source, count, added, *refs):
    parts, terms, outs = refs[:count], refs[count : count + added], refs[count + added :]
    rows = jnp.concatenate([r[...].reshape(-1, D) for r in parts], axis=0)
    if terms:
        rows = rows.astype(F32)
        for t in terms:
            rows = rows + t[...].reshape(-1, D).astype(F32)
        rows = rows.astype(BF16)
    moved = lax.dot_general(
        one_hot(source(columns(ROWS)), ROWS),
        rows,
        (((0,), (0,)), ((), ())),
        preferred_element_type=F32,
    ).astype(BF16)
    start = 0
    for out in outs:
        size = math.prod(out.shape[:-1])
        out[...] = moved[start : start + size].reshape(out.shape)
        start += size


def reorder(parts, source, shapes, terms=()):
    return pl.pallas_call(
        functools.partial(reorder_kernel, source, len(parts), len(terms)),
        out_shape=tuple(jax.ShapeDtypeStruct(shape, BF16) for shape in shapes),
        in_specs=[pl.BlockSpec(memory_space=pltpu.VMEM)] * (len(parts) + len(terms)),
        out_specs=(pl.BlockSpec(memory_space=pltpu.VMEM),) * len(shapes),
        compiler_params=pltpu.CompilerParams(vmem_limit_bytes=16 * 2**20),
        cost_estimate=pl.CostEstimate(flops=170_000_000, bytes_accessed=1_300_000, transcendentals=0),
    )(*parts, *terms)


def weave(n):
    return ((n >> 2) & 1) * 128 + (n >> 3) * 4 + (n & 3)


def unweave(n):
    return ((n >> 2) & 31) * 8 + (n >> 7) * 4 + (n & 3)


def deal(n):
    return ((n >> 2) & 31) * 8 + ((n >> 1) & 1) * 4 + (n >> 7) * 2 + (n & 1)


def undeal(n):
    return ((n >> 1) & 1) * 128 + (n >> 3) * 4 + ((n >> 2) & 1) * 2 + (n & 1)


def collect_kernel(*refs):
    weights, moved, (out, sems) = refs[:-5], refs[-5:-2], refs[-2:]
    p, _ = place()
    copies = []
    for j in range(2):
        for t, w in enumerate(weights):
            sources = [w.at[2 * p + j]] + [m.at[t, j] for m in moved]
            for k, src in enumerate(sources):
                dst = out.at[j, pl.ds((4 * t + k) * HS, HS)]
                copies.append(pltpu.make_async_copy(src, dst, sems.at[j, t, k]))
    for c in copies:
        c.start()
    for c in copies:
        c.wait()


def collect(weights, moved):
    count = len(weights)
    return pl.pallas_call(
        collect_kernel,
        out_shape=jax.ShapeDtypeStruct((2, count * 4 * HS, D), BF16),
        in_specs=[pl.BlockSpec(memory_space=pl.ANY)] * (count + 3),
        out_specs=pl.BlockSpec(memory_space=pltpu.VMEM),
        scratch_shapes=[pltpu.SemaphoreType.DMA((2, count, 4))],
        compiler_params=pltpu.CompilerParams(vmem_limit_bytes=16 * 2**20),
        cost_estimate=pl.CostEstimate(flops=0, bytes_accessed=count * 6_600_000, transcendentals=0),
    )(*in_hbm(weights), *moved)


def run_up(rows, gu):
    gu = lax.dot_general(rows, gu, (((1,), (1,)), ((), ())), preferred_element_type=F32)
    gate, up = gu[:, : 4 * HS], gu[:, 4 * HS :]
    return (gate / (1.0 + jnp.exp(-gate)) * up).astype(BF16)


def experts_kernel(far_low, far_high, own, gu_ref, wd_ref, far_out, own_out):
    for j in range(2):
        rows = jnp.concatenate([far_low[j], far_high[j], own[j]], axis=0)
        act = run_up(rows, gu_ref[j])
        out = jnp.dot(act, wd_ref[j], preferred_element_type=F32).astype(BF16)
        far_out[j] = out[:128]
        own_out[j] = out[128:]


def experts(slots, gu, down):
    return pl.pallas_call(
        experts_kernel,
        out_shape=(jax.ShapeDtypeStruct((2, 128, D), BF16),) * 2,
        in_specs=[pl.BlockSpec(memory_space=pltpu.VMEM)] * 5,
        out_specs=(pl.BlockSpec(memory_space=pltpu.VMEM),) * 2,
        compiler_params=pltpu.CompilerParams(vmem_limit_bytes=24 * 2**20),
        cost_estimate=pl.CostEstimate(
            flops=1_260_000_000, bytes_accessed=2_000_000, transcendentals=327680
        ),
    )(*slots, gu, down)


def add_kernel(a, b, c, out):
    out[...] = a[...].astype(F32) + b[...].astype(F32) + c[...].astype(F32)


def add(a, b, c):
    return pl.pallas_call(
        add_kernel,
        out_shape=jax.ShapeDtypeStruct(a.shape, F32),
        in_specs=[pl.BlockSpec(memory_space=pltpu.VMEM)] * 3,
        out_specs=pl.BlockSpec(memory_space=pltpu.VMEM),
        compiler_params=pltpu.CompilerParams(vmem_limit_bytes=16 * 2**20),
        cost_estimate=pl.CostEstimate(flops=1_260_000_000, bytes_accessed=3_300_000, transcendentals=0),
    )(a, b, c)


def up_kernel(sa, sb, gu_ref, act_ref):
    for j in range(2):
        act_ref[j] = run_up(jnp.concatenate([sa[j], sb[j]], axis=0), gu_ref[j])


def up_half(sa, sb, gu):
    return pl.pallas_call(
        up_kernel,
        out_shape=jax.ShapeDtypeStruct((2, 256, 4 * HS), BF16),
        in_specs=[pl.BlockSpec(memory_space=pltpu.VMEM)] * 3,
        out_specs=pl.BlockSpec(memory_space=pltpu.VMEM),
        compiler_params=pltpu.CompilerParams(vmem_limit_bytes=16 * 2**20),
        cost_estimate=pl.CostEstimate(
            flops=0, bytes_accessed=0, transcendentals=0
        ),
    )(sa, sb, gu)


def down_kernel(act, wd, d1, d3, d2, oa, ob, down_ref, sems):
    p, _ = place()
    copies = []
    for j in range(2):
        for k, src in enumerate((wd.at[2 * p + j], d1.at[0, j], d2.at[0, j], d3.at[0, j])):
            dst = down_ref.at[j, pl.ds(k * HS, HS)]
            copies.append(pltpu.make_async_copy(src, dst, sems.at[j, k]))
    for c in copies:
        c.start()
    for j in range(2):
        for c in copies[4 * j : 4 * (j + 1)]:
            c.wait()
        out = jnp.dot(act[j], down_ref[j], preferred_element_type=F32).astype(BF16)
        oa[j] = out[:128]
        ob[j] = out[128:]


def down_half(act, w_down, downs):
    out = jax.ShapeDtypeStruct((2, 128, D), BF16)
    vmem, anywhere = pl.BlockSpec(memory_space=pltpu.VMEM), pl.BlockSpec(memory_space=pl.ANY)
    return pl.pallas_call(
        down_kernel,
        out_shape=(out, out, jax.ShapeDtypeStruct((2, 4 * HS, D), BF16)),
        in_specs=[vmem] + [anywhere] * 4,
        out_specs=(vmem,) * 3,
        scratch_shapes=[pltpu.SemaphoreType.DMA((2, 4))],
        compiler_params=pltpu.CompilerParams(vmem_limit_bytes=16 * 2**20),
        cost_estimate=pl.CostEstimate(flops=2_520_000_000, bytes_accessed=9_000_000, transcendentals=655360),
    )(act, *in_hbm((w_down,)), *downs)


def body(tokens, router, w_gate, w_up, w_down):
    ups = pack((w_gate, w_up, w_down), tuple((by, (0, 1)) for by in (2, 1, 3)))
    tokens, router, *ups = lax.optimization_barrier((tokens, router, *ups))
    mine, other, comb = front(tokens, router)
    ups = [shift(w, True, by) for w, by in zip(ups, (2, 1, 3))]
    downs = pack((w_gate, w_up, w_down), tuple((by, (2,)) for by in (1, 2, 3)))
    downs = [shift(w, True, by) for w, by in zip(downs, (1, 2, 3))]
    (rows,) = reorder((mine, swap(other)), weave, ((ROWS, D),))
    rows = exchange(rows)
    rows, *ups = lax.optimization_barrier((rows, *ups))
    ups = [ups[n] for n in (1, 0, 2)]
    (s0,) = reorder((rows,), deal, ((2, 128, D),))
    s1, s3 = shift(s0, False, 1), shift(s0, False, 3)
    gu = collect((w_gate, w_up), ups)
    s1, gu = lax.optimization_barrier((s1, gu))
    far = shift(s1[:, :64], False, 1), shift(s3[:, 64:], False, 3)
    o1, o3, down = down_half(up_half(s1, s3, gu), w_down, (downs[0], downs[2], downs[1]))
    t1, t3 = shift(o1, False, 3), shift(o3, False, 1)
    *far, _, _ = lax.optimization_barrier((*far, o1, o3))
    o2, o0 = experts((*far, s0), gu, down)
    t2 = shift(o2, False, 2)
    partial = add(o0, t1, t3)
    (rows,) = reorder((partial,), undeal, ((ROWS, D),), (t2,))
    mine, other = reorder((exchange(rows),), unweave, ((128, D),) * 2)
    rows = jnp.concatenate([mine, swap(other)], axis=0)
    mixed = jnp.dot(comb.reshape(2 * TOK, ROWS), rows, preferred_element_type=F32)
    return mixed.astype(BF16).reshape(2, TOK, D)


def solution(mesh):
    return jax.shard_map(
        body,
        mesh=mesh,
        in_specs=(
            P(("dp", "expert"), None, None),
            P(),
            P("expert", "dp", None),
            P("expert", "dp", None),
            P("expert", "dp", None),
        ),
        out_specs=P(("dp", "expert"), None, None),
        check_vma=False,
    )
```
